32 devices in a mesh: tile: 8 (over z, y), visit: 4 (over x, core).
Axes of the slice: x: 2, y: 2, z: 4, core: 2. Of those that a mesh axis runs over, the one named last changes fastest.
Arguments:
- template: float32 [1024, 2048], P('tile', 'visit'), may hold values from -6 to 6
- row_taps: float32 [16, 21], replicated, may hold values from -1 to 1
- col_taps: float32 [16, 21], replicated, may hold values from -1 to 1
- coeffs: float32 [4, 16, 6], P('visit'), may hold values from -2 to 2
- visits: float32 [4, 1024, 2048], P('visit', 'tile'), may hold values from -6 to 6
- boxes: int32 [4, 2], replicated, may hold values from 0 to 2048, as said below
Outputs:
- difference: float32 [4, 1024, 2048], P('visit', 'tile')
The draws below stay inside these ranges and needn't reach their ends.
Inputs may be any that keep to these rules, and one draw needn't show every extreme that they name: boxes[v, 0] is the first column and boxes[v, 1] the number of columns of visit v's box, which lies within the 2048 columns; boxes[v, 1] is at least 512, and some visit covers all 2048 columns.
All inputs are finite; a program needn't handle non-finite values.
Results may differ from the reference program's by a relative error of at most 0.0003.
Values sent between devices are 32-bit elements; how exact they have to be, the bound alone decides.
A program may use at most 128 MiB of HBM per device.

```python
import jax
import jax.numpy as jnp
from jax import lax

W = 2048
K = 16
TAPS = 21
VISITS = 4
ROWS = 1024


def draw_boxes(key, part):
    first_key, second_key, third_key = jax.random.split(key, 3)
    lengths = jax.random.randint(first_key, (VISITS,), W // 4, W + 1)
    widest = jax.random.randint(second_key, (), 0, VISITS)
    lengths = jnp.where(jnp.arange(VISITS) == widest, W, lengths)
    starts = jax.random.randint(third_key, (VISITS,), 0, W) % (W - lengths + 1)
    return jnp.stack([starts, lengths], axis=1).astype(jnp.int32)


def steps_of(key, dims, cuts, low, largest):
    gain, own = 1.0, jax.random.fold_in(key, 6)
    for position, shards_of in cuts:
        draws = jnp.exp(jax.random.uniform(jax.random.fold_in(own, position), (shards_of,), jnp.float32, low / len(cuts), largest / len(cuts)))
        gain = gain * jnp.repeat(draws, dims[position] // shards_of).reshape([-1 if axis == position else 1 for axis in range(len(dims))])
    return gain


def gaussian(stream_key, dims, width, bound, cuts=(), dtype=jnp.bfloat16):
    loudness = steps_of(stream_key, dims, cuts, -0.22, 0.18) if cuts else 1.0
    entries = jax.random.normal(stream_key, dims, jnp.float32) * width * loudness
    return jnp.minimum(jnp.maximum(entries, -bound), bound).astype(dtype)


def setup_inputs(seed: int = 0) -> dict:
    streams_of = jax.random.split(jax.random.key(seed), 7)
    return {
        "template": gaussian(streams_of[0], (ROWS, W), 1.0, 6.0, ((0, 8), (1, 4)), jnp.float32),
        "row_taps": gaussian(streams_of[1], (K, TAPS), 0.22, 1.0, (), jnp.float32),
        "col_taps": gaussian(streams_of[2], (K, TAPS), 0.22, 1.0, (), jnp.float32),
        "coeffs": gaussian(streams_of[3], (VISITS, K, 6), 0.3, 2.0, ((0, 4),), jnp.float32),
        "visits": gaussian(streams_of[4], (VISITS, ROWS, W), 1.0, 6.0, ((0, 4), (1, 8)), jnp.float32),
        "boxes": draw_boxes(jax.random.fold_in(streams_of[6], 71), 0),
    }


def coordinate(first, count, total):
    return 2.0 * ((first + jnp.arange(count)).astype(jnp.float32) + 0.5) / total - 1.0


def surface_terms(y_coord, x_coord):
    y_grid = y_coord[:, None] * jnp.ones_like(x_coord)[None, :]
    x_grid = jnp.ones_like(y_coord)[:, None] * x_coord[None, :]
    return jnp.stack([jnp.ones_like(x_grid), x_grid, y_grid, x_grid * x_grid, x_grid * y_grid, y_grid * y_grid])


def separable(padded, row_taps, col_taps, tile_rows, span):
    passed = jnp.zeros((row_taps.shape[0], tile_rows, padded.shape[1]), jnp.float32)
    for offset in range(row_taps.shape[1]):
        passed = passed + row_taps[:, offset, None, None] * padded[None, offset:offset + tile_rows, :]
    images = jnp.zeros((row_taps.shape[0], tile_rows, span), jnp.float32)
    for offset in range(col_taps.shape[1]):
        images = images + col_taps[:, offset, None, None] * passed[:, :, offset:offset + span]
    return images


def reference(template, row_taps, col_taps, coeffs, visits, boxes):
    half = TAPS // 2
    padded = jnp.pad(template, half)
    basis = separable(padded, row_taps, col_taps, ROWS, W)
    terms = surface_terms(coordinate(0, ROWS, ROWS), coordinate(0, W, W))
    column_index = jnp.arange(W).astype(jnp.int32)

    def one_visit(packed):
        coef, visit, box = packed
        weighted = jnp.einsum("kt,krc->trc", coef, basis, precision=lax.Precision.HIGHEST)
        model = jnp.sum(weighted * terms, axis=0)
        inside = (column_index >= box[0]) & (column_index < box[0] + box[1])
        return jnp.where(inside[None, :], visit - model, jnp.float32(0.0))

    return lax.map(one_visit, (coeffs, visits, boxes))
```

```python
import functools

import jax
import jax.numpy as jnp
from jax import lax
from jax.experimental import pallas as pl
from jax.experimental.pallas import tpu as pltpu
from jax.sharding import PartitionSpec as P

BLOCK = 64
WINDOW = 96
LANES = 128
CHUNK = 256


def split(value):
    high = value.astype(jnp.bfloat16)
    low = (value - high.astype(jnp.float32)).astype(jnp.bfloat16)
    return high, low


def kernel(taps, rows, columns, total_rows, meta_ref, base_ref, t_ref, vis_ref, out_ref, w_ref, s_ref):
    half = taps // 2
    blocks = rows // BLOCK
    depth = s_ref.shape[2]
    step = pl.program_id(0)

    @pl.when(step == 0)
    def _():
        rolled = [
            pltpu.roll(
                jnp.broadcast_to(base_ref[t : t + 1, :], (BLOCK, depth)), 0, 1, stride=1, stride_axis=0
            )
            for t in range(6)
        ]
        for block in range(blocks):
            row = lax.broadcasted_iota(jnp.int32, (BLOCK, 1), 0) + (meta_ref[0] + block * BLOCK)
            y = 2.0 * (row.astype(jnp.float32) + 0.5) / total_rows - 1.0
            parts = (
                rolled[0] + y * (rolled[2] + y * rolled[5]),
                rolled[1] + y * rolled[4],
                rolled[3],
            )
            for i, part in enumerate(parts):
                high, low = split(part)
                w_ref[0, block, i * BLOCK : (i + 1) * BLOCK, :] = high
                w_ref[1, block, i * BLOCK : (i + 1) * BLOCK, :] = low
        pad = depth - taps * WINDOW
        if pad:
            s_ref[:, :, taps * WINDOW :, :] = jnp.zeros((2, blocks, pad, CHUNK), jnp.bfloat16)

    window = t_ref[:, pl.ds(pl.multiple_of(step * CHUNK, CHUNK), CHUNK + 2 * LANES)]
    for which, part in enumerate(split(window)):
        for b in range(taps):
            first = LANES - half + b
            shifted = part[:, first : first + CHUNK]
            for block in range(blocks):
                s_ref[which, block, b * WINDOW : (b + 1) * WINDOW, :] = shifted[
                    block * BLOCK : block * BLOCK + WINDOW
                ]
    column = lax.broadcasted_iota(jnp.int32, (1, CHUNK), 1) + step * CHUNK
    x = 2.0 * (column.astype(jnp.float32) + 0.5) / columns - 1.0
    inside = (column >= meta_ref[1]) & (column < meta_ref[2])
    for block in range(blocks):
        dot = functools.partial(jnp.dot, preferred_element_type=jnp.float32)
        total = (
            dot(w_ref[0, block], s_ref[0, block])
            + dot(w_ref[1, block], s_ref[0, block])
            + dot(w_ref[0, block], s_ref[1, block])
        )
        model = total[:BLOCK] + x * (total[BLOCK : 2 * BLOCK] + x * total[2 * BLOCK :])
        at = slice(block * BLOCK, (block + 1) * BLOCK)
        out_ref[at, :] = jnp.where(inside, vis_ref[at, :] - model, 0.0)


def bases(coeffs, row_taps, col_taps, depth):
    weight = jnp.sum(
        coeffs.T[:, :, None, None] * col_taps[None, :, :, None] * row_taps[None, :, None, :], axis=1
    )
    taps = row_taps.shape[1]
    base = jnp.pad(weight, ((0, 2), (0, 0), (0, WINDOW - taps))).reshape(8, taps * WINDOW)
    return jnp.pad(base, ((0, 0), (0, depth - taps * WINDOW)))


def local(template, row_taps, col_taps, coeffs, visits, boxes):
    taps = row_taps.shape[1]
    half = taps // 2
    rows, width = template.shape
    columns = width * lax.axis_size("visit")
    count = lax.axis_size("tile")
    blocks = rows // BLOCK
    tall = (blocks - 1) * BLOCK + WINDOW
    depth = -(-taps * WINDOW // 256) * 256
    above = lax.ppermute(template[rows - half :], "tile", [(i, i + 1) for i in range(count - 1)])
    below = lax.ppermute(template[:half], "tile", [(i + 1, i) for i in range(count - 1)])
    slab = jnp.concatenate([above, template, below], axis=0)
    slab = lax.all_gather(slab, "visit", axis=1, tiled=True)
    slab = jnp.pad(slab, ((0, tall - slab.shape[0]), (LANES, LANES)))
    base = bases(coeffs[0], row_taps, col_taps, depth)
    box = lax.dynamic_slice_in_dim(boxes, lax.axis_index("visit"), 1, 0)[0]
    meta = jnp.stack([lax.axis_index("tile").astype(jnp.int32) * rows, box[0], box[0] + box[1]])
    out = pl.pallas_call(
        functools.partial(kernel, taps, rows, columns, rows * count),
        grid=(columns // CHUNK,),
        in_specs=[
            pl.BlockSpec(memory_space=pltpu.SMEM),
            pl.BlockSpec((8, depth), lambda g: (0, 0)),
            pl.BlockSpec((tall, columns + 2 * LANES), lambda g: (0, 0)),
            pl.BlockSpec((rows, CHUNK), lambda g: (0, g)),
        ],
        out_specs=pl.BlockSpec((rows, CHUNK), lambda g: (0, g)),
        out_shape=jax.ShapeDtypeStruct((rows, columns), jnp.float32),
        scratch_shapes=[
            pltpu.VMEM((2, blocks, 3 * BLOCK, depth), jnp.bfloat16),
            pltpu.VMEM((2, blocks, depth, CHUNK), jnp.bfloat16),
        ],
        compiler_params=pltpu.CompilerParams(vmem_limit_bytes=48 * 2**20),
    )(meta, base, slab, visits[0])
    return out[None]


def solution(mesh):
    placed = (P("tile", "visit"), P(), P(), P("visit", None, None), P("visit", "tile", None), P())
    return jax.shard_map(
        local, mesh=mesh, in_specs=placed, out_specs=P("visit", "tile", None), check_vma=False
    )
```

```python
import functools

import jax
import jax.numpy as jnp
from jax import lax
from jax.experimental import pallas as pl
from jax.experimental.pallas import tpu as pltpu
from jax.sharding import PartitionSpec as P

BLOCK = 64
WINDOW = 96
HALO = 16
LANES = 128
CHUNK = 256
MESH = pl.DeviceIdType.MESH


def split(value):
    high = value.astype(jnp.bfloat16)
    low = (value - high.astype(jnp.float32)).astype(jnp.bfloat16)
    return high, low


def kernel(
    tiles, visits, row_ref, col_ref, coeff_ref, boxes_ref, own_ref, vis_ref, out_ref,
    t_ref, w_ref, even_ref, odd_ref, send_sem, recv_sem,
):
    taps = row_ref.shape[1]
    half = taps // 2
    rows, width = own_ref.shape
    columns = width * visits
    steps = columns // CHUNK
    blocks = rows // BLOCK
    depth = w_ref.shape[3]
    tile, visit = lax.axis_index("tile"), lax.axis_index("visit")
    forward = visit < visits // 2
    above, below = tile > 0, tile < tiles - 1

    def span(owner):
        return pl.ds(pl.multiple_of(LANES + owner * width, LANES), width)

    def copy(kind, peer, owner):
        source, first, count, to = (
            (own_ref, HALO, rows, tile),
            (own_ref.at[pl.ds(rows - HALO, HALO)], 0, HALO, tile + 1),
            (own_ref.at[pl.ds(0, HALO)], HALO + rows, HALO, tile - 1),
        )[kind]
        return pltpu.make_async_remote_copy(
            src_ref=source,
            dst_ref=t_ref.at[pl.ds(first, count), span(owner)],
            send_sem=send_sem.at[kind, peer],
            recv_sem=recv_sem.at[kind, owner],
            device_id=(to, peer),
            device_id_type=MESH,
        )

    barrier = pltpu.get_barrier_semaphore()

    def greet(to, peer):
        pl.semaphore_signal(barrier, inc=1, device_id=(to, peer), device_id_type=MESH)

    for offset in range(1, visits):
        greet(tile, lax.rem(visit + offset, visits))
    for allowed, to in ((above, tile - 1), (below, tile + 1)):
        @pl.when(allowed)
        def _():
            for peer in range(visits):
                greet(to, peer)
    beside = jnp.where(above, 1, 0) + jnp.where(below, 1, 0)
    pl.semaphore_wait(barrier, visits - 1 + visits * beside)

    for offset in range(1, visits):
        copy(0, lax.rem(visit + offset, visits), visit).start()
    for kind, allowed in ((1, below), (2, above)):
        @pl.when(allowed)
        def _():
            for peer in range(visits):
                copy(kind, peer, visit).start()

    t_ref[HALO : HALO + rows, span(visit)] = own_ref[...]
    side = jnp.zeros((t_ref.shape[0], LANES), jnp.float32)
    t_ref[:, :LANES] = side
    t_ref[:, LANES + columns :] = side
    for allowed, first in ((above, 0), (below, HALO + rows)):
        @pl.when(jnp.logical_not(allowed))
        def _():
            t_ref[first : first + HALO, LANES : LANES + columns] = jnp.zeros(
                (HALO, columns), jnp.float32
            )

    exact = functools.partial(
        lax.dot_general, precision=lax.Precision.HIGHEST, preferred_element_type=jnp.float32
    )
    place = lax.broadcasted_iota(jnp.int32, (1, depth), 1)
    group = jnp.zeros_like(place)
    for b in range(1, taps + 1):
        group = group + jnp.where(place >= b * WINDOW, 1, 0)
    tap = lax.broadcasted_iota(jnp.int32, (taps, depth), 0)
    in_rows = jnp.where(tap == place - group * WINDOW - (HALO - half), 1.0, 0.0)
    in_cols = jnp.where(tap == group, 1.0, 0.0)
    plain = (((1,), (0,)), ((), ()))
    products = exact(row_ref[...], in_rows, plain) * exact(col_ref[...], in_cols, plain)
    base = exact(coeff_ref[0], products, (((0,), (0,)), ((), ())))
    rolled = [
        pltpu.roll(jnp.broadcast_to(base[t : t + 1], (BLOCK, depth)), 0, 1, stride=1, stride_axis=0)
        for t in range(6)
    ]
    for block in range(blocks):
        row = lax.broadcasted_iota(jnp.int32, (BLOCK, 1), 0) + (tile * rows + block * BLOCK)
        y = 2.0 * (row.astype(jnp.float32) + 0.5) / (rows * tiles) - 1.0
        parts = (
            rolled[0] + y * (rolled[2] + y * rolled[5]),
            rolled[1] + y * rolled[4],
            rolled[3],
        )
        for i, part in enumerate(parts):
            high, low = split(part)
            w_ref[0, block, i * BLOCK : (i + 1) * BLOCK, :] = high
            w_ref[1, block, i * BLOCK : (i + 1) * BLOCK, :] = low
    pad = depth - taps * WINDOW
    if pad:
        for s_ref in (even_ref, odd_ref):
            s_ref[:, :, taps * WINDOW :, :] = jnp.zeros((2, blocks, pad, CHUNK), jnp.bfloat16)

    first_column = boxes_ref[visit, 0]
    end_column = first_column + boxes_ref[visit, 1]

    def chunk_of(step):
        return jnp.where(forward, step, steps - 1 - step)

    def arrive(step):
        for order in range(visits):
            needed = max(0, -(-(order * width - half + 1) // CHUNK) - 1)
            owner = jnp.where(forward, order, visits - 1 - order)
            for kind, allowed in ((0, owner != visit), (1, above), (2, below)):
                @pl.when(jnp.logical_and(step == needed, allowed))
                def _():
                    copy(kind, visit, owner).wait_recv()

    def build(step, s_ref):
        start = pl.multiple_of(chunk_of(step) * CHUNK, CHUNK)
        window = t_ref[:, pl.ds(start, CHUNK + 2 * LANES)]
        for which, part in enumerate(split(window)):
            for b in range(taps):
                first = LANES - half + b
                shifted = part[:, first : first + CHUNK]
                for block in range(blocks):
                    s_ref[which, block, b * WINDOW : (b + 1) * WINDOW, :] = shifted[
                        block * BLOCK : block * BLOCK + WINDOW
                    ]

    def finish(step, s_ref):
        start = pl.multiple_of(chunk_of(step) * CHUNK, CHUNK)
        column = lax.broadcasted_iota(jnp.int32, (1, CHUNK), 1) + start
        x = 2.0 * (column.astype(jnp.float32) + 0.5) / columns - 1.0
        inside = (column >= first_column) & (column < end_column)
        dot = functools.partial(jnp.dot, preferred_element_type=jnp.float32)
        for block in range(blocks):
            total = (
                dot(w_ref[0, block], s_ref[0, block])
                + dot(w_ref[1, block], s_ref[0, block])
                + dot(w_ref[0, block], s_ref[1, block])
            )
            model = total[:BLOCK] + x * (total[BLOCK : 2 * BLOCK] + x * total[2 * BLOCK :])
            at = slice(block * BLOCK, (block + 1) * BLOCK)
            out_ref[at, pl.ds(start, CHUNK)] = jnp.where(
                inside, vis_ref[at, pl.ds(start, CHUNK)] - model, 0.0
            )

    arrive(0)
    build(0, even_ref)

    def pair(index, carry):
        step = 2 * index
        arrive(step + 1)
        build(step + 1, odd_ref)
        finish(step, even_ref)
        arrive(step + 2)
        build(jnp.minimum(step + 2, steps - 1), even_ref)
        finish(step + 1, odd_ref)
        return carry

    lax.fori_loop(0, steps // 2, pair, 0)

    for offset in range(1, visits):
        copy(0, lax.rem(visit + offset, visits), visit).wait_send()
    for kind, allowed in ((1, below), (2, above)):
        @pl.when(allowed)
        def _():
            for peer in range(visits):
                copy(kind, peer, visit).wait_send()


def local(template, row_taps, col_taps, coeffs, visits, boxes):
    taps = row_taps.shape[1]
    rows, width = template.shape
    peers = lax.axis_size("visit")
    columns = width * peers
    blocks = rows // BLOCK
    depth = -(-taps * WINDOW // 256) * 256
    vmem = pl.BlockSpec(memory_space=pltpu.VMEM)
    out = pl.pallas_call(
        functools.partial(kernel, lax.axis_size("tile"), peers),
        in_specs=[vmem, vmem, vmem, pl.BlockSpec(memory_space=pltpu.SMEM), vmem, vmem],
        out_specs=vmem,
        out_shape=jax.ShapeDtypeStruct((rows, columns), jnp.float32),
        scratch_shapes=[
            pltpu.VMEM((rows + 2 * HALO, columns + 2 * LANES), jnp.float32),
            pltpu.VMEM((2, blocks, 3 * BLOCK, depth), jnp.bfloat16),
            pltpu.VMEM((2, blocks, depth, CHUNK), jnp.bfloat16),
            pltpu.VMEM((2, blocks, depth, CHUNK), jnp.bfloat16),
            pltpu.SemaphoreType.DMA((3, peers)),
            pltpu.SemaphoreType.DMA((3, peers)),
        ],
        compiler_params=pltpu.CompilerParams(
            collective_id=0, has_side_effects=True, vmem_limit_bytes=50 * 2**20
        ),
    )(row_taps, col_taps, coeffs, boxes, template, visits[0])
    return out[None]


def solution(mesh):
    placed = (P("tile", "visit"), P(), P(), P("visit", None, None), P("visit", "tile", None), P())
    return jax.shard_map(
        local, mesh=mesh, in_specs=placed, out_specs=P("visit", "tile", None), check_vma=False
    )
```

```python
import functools

import jax
import jax.numpy as jnp
from jax import lax
from jax.experimental import pallas as pl
from jax.experimental.pallas import tpu as pltpu
from jax.sharding import PartitionSpec as P

BLOCK = 64
WINDOW = 96
HALO = 16
LANES = 128
CHUNK = 256
MESH = pl.DeviceIdType.MESH


def split(value):
    high = value.astype(jnp.bfloat16)
    low = (value - high.astype(jnp.float32)).astype(jnp.bfloat16)
    return high, low


def kernel(
    tiles, visits, row_hbm, col_hbm, coeff_hbm, boxes_ref, own_hbm, vis_hbm, out_ref,
    row_ref, col_ref, coeff_ref, vis_ref, t_ref, w_ref, even_ref, odd_ref,
    local_sem, send_sem, recv_sem,
):
    taps = row_ref.shape[1]
    half = taps // 2
    rows, width = own_hbm.shape
    columns = width * visits
    steps = columns // CHUNK
    blocks = rows // BLOCK
    depth = w_ref.shape[2]
    stack = 3 * BLOCK
    tile, visit = lax.axis_index("tile"), lax.axis_index("visit")
    forward = visit < visits // 2
    above, below = tile > 0, tile < tiles - 1
    chips = visits // 2
    core, chip = lax.rem(visit, 2), visit // 2
    partner = chip * 2 + 1 - core
    across = [lax.rem(chip + hop, chips) * 2 + core for hop in range(1, chips)]
    kinds = ((0, None), (1, above), (2, below))
    late = chips == 2 and 2 * width - half >= 2 * CHUNK

    def guarded(condition, action):
        if condition is None:
            action()
        else:
            pl.when(condition)(action)

    def piece(kind, owner):
        first, count = ((HALO, rows), (0, HALO), (HALO + rows, HALO))[kind]
        return t_ref.at[
            pl.ds(first, count), pl.ds(pl.multiple_of(LANES + owner * width, LANES), width)
        ]

    def copy(kind, source, owner, sem, to, peer):
        return pltpu.make_async_remote_copy(
            src_ref=source,
            dst_ref=piece(kind, owner),
            send_sem=sem,
            recv_sem=recv_sem.at[kind, owner],
            device_id=(to, peer),
            device_id_type=MESH,
        )

    def spread(kind, peer):
        source = own_hbm if kind == 0 else piece(kind, visit)
        return copy(kind, source, visit, send_sem.at[kind, peer], tile, peer)

    def edge(kind):
        source = own_hbm.at[pl.ds(rows - HALO if kind == 1 else 0, HALO)]
        to = tile + 1 if kind == 1 else tile - 1
        return copy(kind, source, visit, send_sem.at[kind, visit], to, visit)

    def onward(kind, owner):
        return copy(kind, piece(kind, owner), owner, send_sem.at[3 + kind, owner], tile, partner)

    def arrived(kind, owner):
        copy(kind, piece(kind, owner), owner, send_sem.at[kind, owner], tile, partner).wait_recv()

    loads = [
        pltpu.make_async_copy(source, target, local_sem.at[at])
        for at, (source, target) in enumerate((
            (row_hbm, row_ref), (col_hbm, col_ref), (coeff_hbm, coeff_ref),
            (own_hbm, piece(0, visit)), (vis_hbm, vis_ref),
        ))
    ]
    for load in loads:
        load.start()

    barrier = pltpu.get_barrier_semaphore()

    def greet(to, peer):
        pl.semaphore_signal(barrier, inc=1, device_id=(to, peer), device_id_type=MESH)

    for peer in [*across, partner]:
        greet(tile, peer)
    pl.when(above)(lambda: greet(tile - 1, visit))
    pl.when(below)(lambda: greet(tile + 1, visit))
    beside = jnp.where(above, 1, 0) + jnp.where(below, 1, 0)
    pl.semaphore_wait(barrier, chips + beside)

    pl.when(below)(lambda: edge(1).start())
    pl.when(above)(lambda: edge(2).start())
    for peer in [*across, partner]:
        spread(0, peer).start()

    side = jnp.zeros((t_ref.shape[0], LANES), jnp.float32)
    t_ref[:, :LANES] = side
    t_ref[:, LANES + columns :] = side
    for allowed, first in ((above, 0), (below, HALO + rows)):
        @pl.when(jnp.logical_not(allowed))
        def _():
            t_ref[first : first + HALO, LANES : LANES + columns] = jnp.zeros(
                (HALO, columns), jnp.float32
            )
    for load in loads:
        load.wait()

    exact = functools.partial(
        lax.dot_general, precision=lax.Precision.HIGHEST, preferred_element_type=jnp.float32
    )
    place = lax.broadcasted_iota(jnp.int32, (1, depth), 1)
    group = jnp.zeros_like(place)
    for b in range(1, taps + 1):
        group = group + jnp.where(place >= b * WINDOW, 1, 0)
    tap = lax.broadcasted_iota(jnp.int32, (taps, depth), 0)
    in_rows = jnp.where(tap == place - group * WINDOW - (HALO - half), 1.0, 0.0)
    in_cols = jnp.where(tap == group, 1.0, 0.0)
    plain = (((1,), (0,)), ((), ()))
    products = exact(row_ref[...], in_rows, plain) * exact(col_ref[...], in_cols, plain)
    base = exact(coeff_ref[0], products, (((0,), (0,)), ((), ())))
    for kind, allowed in kinds[1:]:
        @pl.when(allowed)
        def _():
            arrived(kind, visit)
            for peer in [*across, partner]:
                spread(kind, peer).start()
    rolled = [
        pltpu.roll(jnp.broadcast_to(base[t : t + 1], (BLOCK, depth)), 0, 1, stride=1, stride_axis=0)
        for t in range(6)
    ]
    for block in range(blocks):
        row = lax.broadcasted_iota(jnp.int32, (BLOCK, 1), 0) + (tile * rows + block * BLOCK)
        y = 2.0 * (row.astype(jnp.float32) + 0.5) / (rows * tiles) - 1.0
        parts = (
            rolled[0] + y * (rolled[2] + y * rolled[5]),
            rolled[1] + y * rolled[4],
            rolled[3],
        )
        for i, part in enumerate(parts):
            high, low = split(part)
            w_ref[block, i * BLOCK : (i + 1) * BLOCK, :] = high
            w_ref[block, stack + i * BLOCK : stack + (i + 1) * BLOCK, :] = low
    pad = depth - taps * WINDOW
    if pad:
        for s_ref in (even_ref, odd_ref):
            s_ref[:, :, taps * WINDOW :, :] = jnp.zeros((2, blocks, pad, CHUNK), jnp.bfloat16)

    first_column = boxes_ref[visit, 0]
    end_column = first_column + boxes_ref[visit, 1]

    def chunk_of(step):
        return jnp.where(forward, step, steps - 1 - step)

    def arrive(step):
        for order in range(visits):
            needed = max(0, -(-(order * width - half + 1) // CHUNK) - 1)
            owner = jnp.where(forward, order, visits - 1 - order)
            for kind, allowed in kinds:
                here = jnp.logical_and(step == needed, lax.rem(owner, 2) != core)
                if allowed is not None:
                    here = jnp.logical_and(here, allowed)
                pl.when(here)(functools.partial(arrived, kind, owner))

    def relay():
        for owner in across:
            for kind, allowed in kinds:
                def pass_on():
                    arrived(kind, owner)
                    onward(kind, owner).start()
                guarded(allowed, pass_on)

    def build(step, s_ref):
        start = pl.multiple_of(chunk_of(step) * CHUNK, CHUNK)
        window = t_ref[:, pl.ds(start, CHUNK + 2 * LANES)]
        for which, part in enumerate(split(window)):
            for b in range(taps):
                first = LANES - half + b
                shifted = part[:, first : first + CHUNK]
                for block in range(blocks):
                    s_ref[which, block, b * WINDOW : (b + 1) * WINDOW, :] = shifted[
                        block * BLOCK : block * BLOCK + WINDOW
                    ]

    def finish(step, s_ref):
        start = pl.multiple_of(chunk_of(step) * CHUNK, CHUNK)
        column = lax.broadcasted_iota(jnp.int32, (1, CHUNK), 1) + start
        x = 2.0 * (column.astype(jnp.float32) + 0.5) / columns - 1.0
        inside = (column >= first_column) & (column < end_column)
        dot = functools.partial(jnp.dot, preferred_element_type=jnp.float32)
        for block in range(blocks):
            both = dot(w_ref[block], s_ref[0, block])
            total = both[:stack] + both[stack:] + dot(w_ref[block, :stack], s_ref[1, block])
            model = total[:BLOCK] + x * (total[BLOCK : 2 * BLOCK] + x * total[2 * BLOCK :])
            at = slice(block * BLOCK, (block + 1) * BLOCK)
            out_ref[at, pl.ds(start, CHUNK)] = jnp.where(
                inside, vis_ref[at, pl.ds(start, CHUNK)] - model, 0.0
            )

    if not late:
        relay()
    arrive(0)
    build(0, even_ref)

    def pair(index, carry):
        step = 2 * index
        arrive(step + 1)
        build(step + 1, odd_ref)
        finish(step, even_ref)
        if late:
            pl.when(index == 0)(relay)
        arrive(step + 2)
        build(jnp.minimum(step + 2, steps - 1), even_ref)
        finish(step + 1, odd_ref)
        return carry

    lax.fori_loop(0, steps // 2, pair, 0)

    pl.when(below)(lambda: edge(1).wait_send())
    pl.when(above)(lambda: edge(2).wait_send())
    for kind, allowed in kinds:
        def sent():
            for peer in [*across, partner]:
                spread(kind, peer).wait_send()
            for owner in across:
                onward(kind, owner).wait_send()
        guarded(allowed, sent)


def local(template, row_taps, col_taps, coeffs, visits, boxes):
    taps = row_taps.shape[1]
    rows, width = template.shape
    peers = lax.axis_size("visit")
    columns = width * peers
    blocks = rows // BLOCK
    depth = -(-taps * WINDOW // 256) * 256
    hbm = pl.BlockSpec(memory_space=pltpu.HBM)
    out = pl.pallas_call(
        functools.partial(kernel, lax.axis_size("tile"), peers),
        in_specs=[hbm, hbm, hbm, pl.BlockSpec(memory_space=pltpu.SMEM), hbm, hbm],
        out_specs=pl.BlockSpec(memory_space=pltpu.VMEM),
        out_shape=jax.ShapeDtypeStruct((rows, columns), jnp.float32),
        scratch_shapes=[
            pltpu.VMEM(row_taps.shape, jnp.float32),
            pltpu.VMEM(col_taps.shape, jnp.float32),
            pltpu.VMEM(coeffs.shape, jnp.float32),
            pltpu.VMEM((rows, columns), jnp.float32),
            pltpu.VMEM((rows + 2 * HALO, columns + 2 * LANES), jnp.float32),
            pltpu.VMEM((blocks, 6 * BLOCK, depth), jnp.bfloat16),
            pltpu.VMEM((2, blocks, depth, CHUNK), jnp.bfloat16),
            pltpu.VMEM((2, blocks, depth, CHUNK), jnp.bfloat16),
            pltpu.SemaphoreType.DMA((5,)),
            pltpu.SemaphoreType.DMA((6, peers)),
            pltpu.SemaphoreType.DMA((3, peers)),
        ],
        compiler_params=pltpu.CompilerParams(
            collective_id=0, has_side_effects=True, vmem_limit_bytes=62 * 2**20
        ),
    )(row_taps, col_taps, coeffs, boxes, template, visits[0])
    return out[None]


def solution(mesh):
    placed = (P("tile", "visit"), P(), P(), P("visit", None, None), P("visit", "tile", None), P())
    return jax.shard_map(
        local, mesh=mesh, in_specs=placed, out_specs=P("visit", "tile", None), check_vma=False
    )
```

```python
import functools

import jax
import jax.numpy as jnp
from jax import lax
from jax.experimental import pallas as pl
from jax.experimental.pallas import tpu as pltpu
from jax.sharding import PartitionSpec as P

BLOCK = 64
WINDOW = 96
HALO = 16
LANES = 128
CHUNK = 256
MESH = pl.DeviceIdType.MESH


def split(value):
    high = value.astype(jnp.bfloat16)
    low = (value - high.astype(jnp.float32)).astype(jnp.bfloat16)
    return high, low


def kernel(
    tiles, visits, row_hbm, col_hbm, coeff_hbm, own_hbm, out_ref,
    row_ref, col_ref, coeff_ref, t_ref, w_ref, even_ref, odd_ref,
    local_sem, send_sem, recv_sem,
):
    taps = row_ref.shape[1]
    half = taps // 2
    rows, width = own_hbm.shape
    columns = width * visits
    steps = columns // CHUNK
    blocks = rows // BLOCK
    depth = w_ref.shape[2]
    stack = 3 * BLOCK
    tile, visit = lax.axis_index("tile"), lax.axis_index("visit")
    forward = visit < visits // 2
    above, below = tile > 0, tile < tiles - 1
    chips = visits // 2
    core, chip = lax.rem(visit, 2), visit // 2
    partner = chip * 2 + 1 - core
    across = [lax.rem(chip + hop, chips) * 2 + core for hop in range(1, chips)]
    kinds = ((0, None), (1, above), (2, below))
    late = chips == 2 and 2 * width - half >= 2 * CHUNK

    def guarded(condition, action):
        if condition is None:
            action()
        else:
            pl.when(condition)(action)

    def piece(kind, owner):
        first, count = ((HALO, rows), (0, HALO), (HALO + rows, HALO))[kind]
        return t_ref.at[
            pl.ds(first, count), pl.ds(pl.multiple_of(LANES + owner * width, LANES), width)
        ]

    def copy(kind, source, owner, sem, to, peer):
        return pltpu.make_async_remote_copy(
            src_ref=source,
            dst_ref=piece(kind, owner),
            send_sem=sem,
            recv_sem=recv_sem.at[kind, owner],
            device_id=(to, peer),
            device_id_type=MESH,
        )

    def spread(kind, peer):
        source = own_hbm if kind == 0 else piece(kind, visit)
        return copy(kind, source, visit, send_sem.at[kind, peer], tile, peer)

    def edge(kind):
        source = own_hbm.at[pl.ds(rows - HALO if kind == 1 else 0, HALO)]
        to = tile + 1 if kind == 1 else tile - 1
        return copy(kind, source, visit, send_sem.at[kind, visit], to, visit)

    def onward(kind, owner):
        return copy(kind, piece(kind, owner), owner, send_sem.at[3 + kind, owner], tile, partner)

    def arrived(kind, owner):
        copy(kind, piece(kind, owner), owner, send_sem.at[kind, owner], tile, partner).wait_recv()

    loads = [
        pltpu.make_async_copy(source, target, local_sem.at[at])
        for at, (source, target) in enumerate((
            (row_hbm, row_ref), (col_hbm, col_ref), (coeff_hbm, coeff_ref),
            (own_hbm, piece(0, visit)),
        ))
    ]
    for load in loads:
        load.start()

    barrier = pltpu.get_barrier_semaphore()

    def greet(to, peer):
        pl.semaphore_signal(barrier, inc=1, device_id=(to, peer), device_id_type=MESH)

    for peer in [*across, partner]:
        greet(tile, peer)
    pl.when(above)(lambda: greet(tile - 1, visit))
    pl.when(below)(lambda: greet(tile + 1, visit))
    beside = jnp.where(above, 1, 0) + jnp.where(below, 1, 0)
    pl.semaphore_wait(barrier, chips + beside)

    pl.when(below)(lambda: edge(1).start())
    pl.when(above)(lambda: edge(2).start())
    for peer in [*across, partner]:
        spread(0, peer).start()

    side = jnp.zeros((t_ref.shape[0], LANES), jnp.float32)
    t_ref[:, :LANES] = side
    t_ref[:, LANES + columns :] = side
    for allowed, first in ((above, 0), (below, HALO + rows)):
        @pl.when(jnp.logical_not(allowed))
        def _():
            t_ref[first : first + HALO, LANES : LANES + columns] = jnp.zeros(
                (HALO, columns), jnp.float32
            )
    for load in loads:
        load.wait()

    exact = functools.partial(
        lax.dot_general, precision=lax.Precision.HIGHEST, preferred_element_type=jnp.float32
    )
    place = lax.broadcasted_iota(jnp.int32, (1, depth), 1)
    group = jnp.zeros_like(place)
    for b in range(1, taps + 1):
        group = group + jnp.where(place >= b * WINDOW, 1, 0)
    tap = lax.broadcasted_iota(jnp.int32, (taps, depth), 0)
    in_rows = jnp.where(tap == place - group * WINDOW - (HALO - half), 1.0, 0.0)
    in_cols = jnp.where(tap == group, 1.0, 0.0)
    plain = (((1,), (0,)), ((), ()))
    products = exact(row_ref[...], in_rows, plain) * exact(col_ref[...], in_cols, plain)
    base = exact(coeff_ref[:, 0, :], products, plain)
    for kind, allowed in kinds[1:]:
        @pl.when(allowed)
        def _():
            arrived(kind, visit)
            for peer in [*across, partner]:
                spread(kind, peer).start()
    rolled = [
        pltpu.roll(jnp.broadcast_to(base[t : t + 1], (BLOCK, depth)), 0, 1, stride=1, stride_axis=0)
        for t in range(6)
    ]
    for block in range(blocks):
        row = lax.broadcasted_iota(jnp.int32, (BLOCK, 1), 0) + (tile * rows + block * BLOCK)
        y = 2.0 * (row.astype(jnp.float32) + 0.5) / (rows * tiles) - 1.0
        parts = (
            rolled[0] + y * (rolled[2] + y * rolled[5]),
            rolled[1] + y * rolled[4],
            rolled[3],
        )
        for i, part in enumerate(parts):
            high, low = split(part)
            w_ref[block, i * BLOCK : (i + 1) * BLOCK, :] = high
            w_ref[block, stack + i * BLOCK : stack + (i + 1) * BLOCK, :] = low
    pad = depth - taps * WINDOW
    if pad:
        for s_ref in (even_ref, odd_ref):
            s_ref[:, :, taps * WINDOW :, :] = jnp.zeros((2, blocks, pad, CHUNK), jnp.bfloat16)

    def chunk_of(step):
        return jnp.where(forward, step, steps - 1 - step)

    def arrive(step):
        for order in range(visits):
            needed = max(0, -(-(order * width - half + 1) // CHUNK) - 1)
            owner = jnp.where(forward, order, visits - 1 - order)
            for kind, allowed in kinds:
                here = jnp.logical_and(step == needed, lax.rem(owner, 2) != core)
                if allowed is not None:
                    here = jnp.logical_and(here, allowed)
                pl.when(here)(functools.partial(arrived, kind, owner))

    def relay():
        for owner in across:
            for kind, allowed in kinds:
                def pass_on():
                    arrived(kind, owner)
                    onward(kind, owner).start()
                guarded(allowed, pass_on)

    def build(step, s_ref):
        start = pl.multiple_of(chunk_of(step) * CHUNK, CHUNK)
        window = t_ref[:, pl.ds(start, CHUNK + 2 * LANES)]
        for which, part in enumerate(split(window)):
            for b in range(taps):
                first = LANES - half + b
                shifted = part[:, first : first + CHUNK]
                for block in range(blocks):
                    s_ref[which, block, b * WINDOW : (b + 1) * WINDOW, :] = shifted[
                        block * BLOCK : block * BLOCK + WINDOW
                    ]

    def finish(step, s_ref):
        start = pl.multiple_of(chunk_of(step) * CHUNK, CHUNK)
        column = lax.broadcasted_iota(jnp.int32, (1, CHUNK), 1) + start
        x = 2.0 * (column.astype(jnp.float32) + 0.5) / columns - 1.0
        dot = functools.partial(jnp.dot, preferred_element_type=jnp.float32)
        for block in range(blocks):
            both = dot(w_ref[block], s_ref[0, block])
            total = both[:stack] + both[stack:] + dot(w_ref[block, :stack], s_ref[1, block])
            model = total[:BLOCK] + x * (total[BLOCK : 2 * BLOCK] + x * total[2 * BLOCK :])
            at = slice(block * BLOCK, (block + 1) * BLOCK)
            out_ref[at, pl.ds(start, CHUNK)] = model

    if not late:
        relay()
    arrive(0)
    build(0, even_ref)

    def pair(index, carry):
        step = 2 * index
        arrive(step + 1)
        build(step + 1, odd_ref)
        finish(step, even_ref)
        if late:
            pl.when(index == 0)(relay)
        arrive(step + 2)
        build(jnp.minimum(step + 2, steps - 1), even_ref)
        finish(step + 1, odd_ref)
        return carry

    lax.fori_loop(0, steps // 2, pair, 0)

    pl.when(below)(lambda: edge(1).wait_send())
    pl.when(above)(lambda: edge(2).wait_send())
    for kind, allowed in kinds:
        def sent():
            for peer in [*across, partner]:
                spread(kind, peer).wait_send()
            for owner in across:
                onward(kind, owner).wait_send()
        guarded(allowed, sent)


def local(template, row_taps, col_taps, coeffs, visits, boxes):
    taps = row_taps.shape[1]
    rows, width = template.shape
    peers = lax.axis_size("visit")
    columns = width * peers
    blocks = rows // BLOCK
    depth = -(-taps * WINDOW // 256) * 256
    hbm = pl.BlockSpec(memory_space=pltpu.HBM)
    model = pl.pallas_call(
        functools.partial(kernel, lax.axis_size("tile"), peers),
        in_specs=[hbm] * 4,
        out_specs=pl.BlockSpec(memory_space=pltpu.VMEM),
        out_shape=jax.ShapeDtypeStruct((rows, columns), jnp.float32),
        scratch_shapes=[
            pltpu.VMEM(row_taps.shape, jnp.float32),
            pltpu.VMEM(col_taps.shape, jnp.float32),
            pltpu.VMEM((coeffs.shape[2], 1, coeffs.shape[1]), jnp.float32),
            pltpu.VMEM((rows + 2 * HALO, columns + 2 * LANES), jnp.float32),
            pltpu.VMEM((blocks, 6 * BLOCK, depth), jnp.bfloat16),
            pltpu.VMEM((2, blocks, depth, CHUNK), jnp.bfloat16),
            pltpu.VMEM((2, blocks, depth, CHUNK), jnp.bfloat16),
            pltpu.SemaphoreType.DMA((4,)),
            pltpu.SemaphoreType.DMA((6, peers)),
            pltpu.SemaphoreType.DMA((3, peers)),
        ],
        compiler_params=pltpu.CompilerParams(
            collective_id=0, has_side_effects=True, vmem_limit_bytes=62 * 2**20
        ),
    )(row_taps, col_taps, coeffs.transpose(2, 0, 1), template)
    box = lax.dynamic_slice_in_dim(boxes, lax.axis_index("visit"), 1, 0)
    column = jnp.arange(columns)[None, :]
    inside = (column >= box[:, 0:1]) & (column < box[:, 0:1] + box[:, 1:2])
    return jnp.where(inside[:, None, :], visits - model[None], jnp.float32(0.0))


def solution(mesh):
    placed = (P("tile", "visit"), P(), P(), P("visit", None, None), P("visit", "tile", None), P())
    return jax.shard_map(
        local, mesh=mesh, in_specs=placed, out_specs=P("visit", "tile", None), check_vma=False
    )
```
